32 devices in a mesh: fsdp: 2 (over x), tok: 16 (over z, y, core).
Axes of the slice: x: 2, y: 2, z: 4, core: 2. Of those that a mesh axis runs over, the one named last changes fastest.
Arguments:
- queries: bfloat16 [2, 2048, 3072], P('fsdp', 'tok'), may hold values from -6 to 6
- keys: bfloat16 [2, 2048, 3072], P('fsdp', 'tok'), may hold values from -6 to 6
- values: bfloat16 [2, 2048, 3072], P('fsdp', 'tok'), may hold values from -6 to 6
- readout: bfloat16 [3072, 1000], P('fsdp'), may hold values from -12 to 12
- global_block: int32 [2], P('fsdp'), may hold values from 0 to 15
- q_gain: float32 [3072], replicated, may hold values from 0.5 to 5
- k_gain: float32 [3072], replicated, may hold values from 0.5 to 5
Outputs:
- entropy: float32 [], replicated
- q_grad: float32 [3072], replicated
- k_grad: float32 [3072], replicated
The draws below stay inside these ranges and needn't reach their ends.
All inputs are finite; a program needn't handle non-finite values.
Results may differ from the reference program's by a relative error of at most 0.02.
The reference program's roundings to bfloat16 on the way (of `attention`) count: a program that leaves them out, or rounds other values in their place, can miss the bound.
Values may be sent and summed in bfloat16 or wider, within the bound.
No kernel may reach another device: no remote copies, remote signals or barrier semaphores. Data moves between devices by JAX's collectives and lax.ppermute only.
A program may use at most 64 MiB of HBM per device.

```python
import jax
import jax.numpy as jnp
from jax import lax

HEADS = 24
HEAD = 128
CLASSES = 1000
ROW = 64
GBLK = 128
TOK_DEV = 128
VIEWS = 2
TOKENS_VIEW = 2048
NBLK = 16
N_TOK = 16


def shared_keys(key):
    return jax.random.truncated_normal(jax.random.fold_in(key, 7), -6.0, 6.0, (VIEWS, TOKENS_VIEW, HEADS * HEAD), jnp.float32)


def draw_keys(key, part):
    return shared_keys(key).astype(jnp.bfloat16)


def draw_queries(key, part):
    fresh = jax.random.truncated_normal(jax.random.fold_in(key, 11), -6.0, 6.0, (VIEWS, TOKENS_VIEW, HEADS * HEAD), jnp.float32)
    return fresh.astype(jnp.bfloat16)


def draw_q_gain(key, part):
    uniform_part = jax.random.uniform(jax.random.fold_in(key, 13), (HEADS * HEAD,), jnp.float32)
    return 0.5 * jnp.power(4.0, uniform_part)


def draw_k_gain(key, part):
    uniform_part = jax.random.uniform(jax.random.fold_in(key, 17), (HEADS * HEAD,), jnp.float32)
    return 0.5 * jnp.power(4.0, uniform_part)


def block_levels(own_key, dims, split, smallest, largest):
    def one(axis_at, blocks):
        steps = jax.random.uniform(jax.random.fold_in(jax.random.fold_in(own_key, 6), axis_at), (blocks,), jnp.float32, smallest / len(split), largest / len(split))
        return jnp.repeat(jnp.exp(steps), dims[axis_at] // blocks).reshape((-1,) + (1,) * (len(dims) - axis_at - 1))

    level = one(*split[0])
    for cut in split[1:]:
        level = level * one(*cut)
    return level


def normal_values(own_key, extent, width, limit, cuts=(), held_as=jnp.bfloat16):
    level = block_levels(own_key, extent, cuts, -0.22, 0.18) if cuts else 1.0
    values = jax.random.normal(own_key, extent, jnp.float32) * width * level
    return jnp.minimum(jnp.maximum(values, -limit), limit).astype(held_as)


def setup_inputs(seed: int = 0) -> dict:
    arg_keys = jax.random.split(jax.random.key(seed), 8)
    queries = draw_queries(jax.random.fold_in(arg_keys[7], 71), 0)
    keys = draw_keys(jax.random.fold_in(arg_keys[7], 71), 0)
    values = normal_values(arg_keys[2], (VIEWS, TOKENS_VIEW, HEADS * HEAD), 1.0, 6.0, ((0, 2), (1, 16)))
    readout = normal_values(arg_keys[3], (HEADS * HEAD, CLASSES), 2.0, 12.0, ((0, 2),))
    global_block = jax.random.randint(arg_keys[4], (VIEWS,), 0, NBLK).astype(jnp.int32)
    q_gain = draw_q_gain(jax.random.fold_in(arg_keys[7], 71), 0)
    k_gain = draw_k_gain(jax.random.fold_in(arg_keys[7], 71), 0)
    return dict(queries=queries, keys=keys, values=values, readout=readout, global_block=global_block, q_gain=q_gain, k_gain=k_gain)


def normalize(entries, gain):
    entries = entries.astype(jnp.float32)
    average = lax.optimization_barrier(jnp.mean(entries, -1, keepdims=True))
    centred = entries - average
    variance = lax.optimization_barrier(jnp.mean(centred * centred, -1, keepdims=True))
    return (centred * lax.rsqrt(variance + 1e-06) * gain).astype(jnp.bfloat16)

def group_total(query_part, key_part, value_part, usable, gain_query, gain_key):
    query_norm = normalize(query_part, gain_query)
    key_norm = normalize(key_part, gain_key)
    scores = jnp.einsum('qhd,khd->hqk', query_norm, key_norm, preferred_element_type=jnp.float32) * HEAD ** (-0.5)
    scores = jnp.where(usable[None, None, :], scores, -1e+30)
    row_max = lax.optimization_barrier(jnp.max(scores, -1, keepdims=True))
    exponent = jnp.exp(scores - row_max)
    row_total = lax.optimization_barrier(jnp.sum(exponent, -1, keepdims=True))
    attention = (exponent / row_total).astype(jnp.bfloat16)
    return jnp.einsum('hqk,khd->hd', attention, value_part, preferred_element_type=jnp.float32)

def attend_sum(query_rows, context, usable, gain_query, gain_key, group_size):
    head_count = gain_query.shape[0] // HEAD
    query_heads = query_rows.reshape(query_rows.shape[0], head_count, HEAD)
    key_heads = context[0].reshape(context.shape[1], head_count, HEAD)
    value_heads = context[1].reshape(context.shape[1], head_count, HEAD)
    query_gains = gain_query.reshape(head_count, HEAD)
    key_gains = gain_key.reshape(head_count, HEAD)
    if group_size == head_count:
        return group_total(query_heads, key_heads, value_heads, usable, query_gains, key_gains).reshape(-1)
    checked = jax.checkpoint(group_total)

    def per_group(group_index):
        first_head = (group_index * group_size).astype(jnp.int32)
        return checked(lax.dynamic_slice_in_dim(query_heads, first_head, group_size, 1), lax.dynamic_slice_in_dim(key_heads, first_head, group_size, 1), lax.dynamic_slice_in_dim(value_heads, first_head, group_size, 1), usable, lax.dynamic_slice_in_dim(query_gains, first_head, group_size, 0), lax.dynamic_slice_in_dim(key_gains, first_head, group_size, 0))
    return lax.map(per_group, jnp.arange(head_count // group_size, dtype=jnp.int32)).reshape(-1)

def reference(queries, keys, values, readout, global_block, q_gain, k_gain):

    def loss_of(gain_query, gain_key):

        def per_view(view_index):
            query_view = lax.dynamic_index_in_dim(queries, view_index, 0, False)
            key_view = lax.dynamic_index_in_dim(keys, view_index, 0, False)
            value_view = lax.dynamic_index_in_dim(values, view_index, 0, False)
            key_value = jnp.stack([key_view, value_view])
            padded = jnp.pad(key_value, ((0, 0), (ROW, ROW), (0, 0)))
            global_id = lax.dynamic_index_in_dim(global_block, view_index, 0, False).astype(jnp.int32)
            shared = lax.dynamic_slice_in_dim(key_value, (global_id * GBLK).astype(jnp.int32), GBLK, 1)

            def per_band(band_index):
                first_row = (band_index * TOK_DEV).astype(jnp.int32)
                own_rows = lax.dynamic_slice_in_dim(key_value, first_row, TOK_DEV, 1)
                lower_rows = lax.dynamic_slice_in_dim(padded, first_row, ROW, 1)
                upper_rows = lax.dynamic_slice_in_dim(padded, (first_row + ROW + TOK_DEV).astype(jnp.int32), ROW, 1)
                context = jnp.concatenate([own_rows, lower_rows, upper_rows, shared], axis=1)
                usable = jnp.concatenate([jnp.ones((TOK_DEV,), bool), jnp.full((ROW,), band_index > 0), jnp.full((ROW,), band_index < N_TOK - 1), jnp.ones((GBLK,), bool)])
                query_rows = lax.dynamic_slice_in_dim(query_view, first_row, TOK_DEV, 0)
                return attend_sum(query_rows, context, usable, gain_query, gain_key, HEADS)
            return lax.optimization_barrier(jnp.sum(lax.map(jax.checkpoint(per_band), jnp.arange(N_TOK, dtype=jnp.int32)), 0))
        sums = lax.map(jax.checkpoint(per_view), jnp.arange(VIEWS, dtype=jnp.int32))
        pooled = sums / TOKENS_VIEW
        logits = jnp.dot(pooled, readout.astype(jnp.float32), precision=lax.Precision.HIGHEST)
        view_probs = jax.nn.softmax(logits, -1)
        mean_probs = lax.optimization_barrier(jnp.mean(view_probs, 0))
        return -jnp.sum(mean_probs * jnp.log(mean_probs))
    entropy, gradients = jax.value_and_grad(loss_of, argnums=(0, 1))(q_gain, k_gain)
    return (entropy, gradients[0], gradients[1])
```

```python
import functools

import jax
import jax.numpy as jnp
from jax import lax
from jax.experimental import pallas as pl
from jax.experimental.pallas import tpu as pltpu
from jax.sharding import Mesh, PartitionSpec as P

HEAD = 128
ROW = 64
GBLK = 128
GROUP = 4
PER = 6
STEP = 2
NEG = -1e30
SCALE = HEAD**-0.5
LOG2E = 1.4426950408889634
F32 = jnp.float32
BF16 = jnp.bfloat16
VMEM = pl.BlockSpec(memory_space=pltpu.VMEM)
SMEM = pl.BlockSpec(memory_space=pltpu.SMEM)
PARAMS = pltpu.CompilerParams(vmem_limit_bytes=16 * 1024 * 1024)
ALONE = pltpu.CompilerParams(vmem_limit_bytes=63 * 1024 * 1024)
HBM = pl.BlockSpec(memory_space=pltpu.HBM)

NN = (((1,), (0,)), ((), ()))
NT = (((1,), (1,)), ((), ()))

SHARES = (0, 2, 1, 3)


def dot(a, b, dims):
    return lax.dot_general(a, b, dims, preferred_element_type=F32)


def two(x):
    zero = jnp.zeros_like(x[0])
    return jnp.concatenate(
        [jnp.concatenate([x[0], zero], axis=1), jnp.concatenate([zero, x[1]], axis=1)], axis=0
    )


def centring():
    row = lax.broadcasted_iota(jnp.int32, (HEAD, HEAD), 0)
    col = lax.broadcasted_iota(jnp.int32, (HEAD, HEAD), 1)
    centre = ((row == col).astype(F32) - 1.0 / HEAD).astype(BF16)
    return two((centre, centre)), two(((row == col).astype(F32).astype(BF16),) * 2)


def unit_rows(x, centre):
    x = dot(x, centre, NN)
    parts = []
    for i in range(2):
        part = x[:, i * HEAD:(i + 1) * HEAD]
        variance = jnp.sum(part * part, axis=1, keepdims=True) * (1.0 / HEAD)
        parts.append(part * lax.rsqrt(variance + 1e-06))
    return jnp.concatenate(parts, axis=1)


def thirds(x):
    a = x.astype(BF16)
    rest = x - a.astype(F32)
    b = rest.astype(BF16)
    c = (rest - b.astype(F32)).astype(BF16)
    pad = jnp.zeros((13, x.shape[1]), BF16)
    return jnp.concatenate([a, b, c, pad], axis=0)


def two_heads(q, keys, values, gain_q, gain_k, edge):
    centre, eye = centring()
    tile = lambda x, t: x[t * HEAD:(t + 1) * HEAD]
    side = lambda x, i: x[:, i * HEAD:(i + 1) * HEAD]
    beside = lambda *parts: jnp.concatenate(parts, axis=1)
    below = lambda *parts: jnp.concatenate(parts, axis=0)
    qn, qnt, qns = [], [], []
    for t in range(GROUP):
        qn.append((unit_rows(tile(q, t), centre) * gain_q).astype(BF16))
        x = jnp.transpose(qn[t])
        qns.append(x)
        qnt.append(two((tile(x, 0), tile(x, 1))))
    kn = [(unit_rows(tile(keys, t), centre) * gain_k).astype(BF16) for t in range(GROUP + 2)]

    last = GROUP + 1
    attn = []
    for b in range(GROUP):
        scores = dot(below(kn[b], kn[b + 1], kn[last]), qnt[b], NN)
        if b == 0:
            scores = below(scores[:ROW] + edge[0], scores[ROW:])
        if b == GROUP - 1:
            at = 2 * HEAD
            scores = below(scores[:at - ROW], scores[at - ROW:at] + edge[1], scores[at:])
        top = jnp.max(scores, axis=0, keepdims=True)
        expo = jnp.exp2((scores - top) * (SCALE * LOG2E))
        attn.append((expo * (1.0 / jnp.sum(expo, axis=0, keepdims=True))).astype(BF16))

    knt = [jnp.transpose(x) for x in kn]
    vt = dot(eye, values, NT).astype(BF16)
    vt = [side(vt, t) for t in range(GROUP + 2)]
    zero = jnp.zeros((HEAD, HEAD), BF16)
    results = []
    for i in range(2):
        both = [below(tile(knt[t], i), tile(vt[t], i)) for t in range(GROUP + 2)]
        back = [None] * (GROUP + 2)
        outs, negs = [], []
        for b in range(0, GROUP, 2):
            one, other = side(attn[b], i), side(attn[b + 1], i)
            pair = below(
                beside(tile(one, 0), zero),
                beside(tile(one, 1), tile(other, 0)),
                beside(zero, tile(other, 1)),
                beside(tile(one, 2), tile(other, 2)),
            )
            made = dot(beside(both[b], both[b + 1], both[b + 2], both[last]), pair, NN)
            queries = below(side(qn[b], i), side(qn[b + 1], i))
            outs.append(made[HEAD:])
            negs.append(beside(tile(qns[b], i), tile(qns[b + 1], i)) * made[:HEAD].astype(BF16))
            moved = dot(pair, queries, NN)
            for n, t in enumerate((b, b + 1, b + 2, last)):
                piece = tile(moved, n)
                back[t] = piece if back[t] is None else back[t] + piece
        moved = [side(kn[t], i) * back[t].astype(BF16) for t in range(GROUP + 2)]
        jac = dot(beside(*[tile(v, i) for v in vt]), below(*moved), NN)
        jac = jac - dot(beside(*[o.astype(BF16) for o in outs]), beside(*negs), NT)
        sums = outs[0] + outs[1]
        sums = side(sums, 0) + side(sums, 1)
        results.append((jnp.sum(jnp.transpose(sums), axis=0, keepdims=True), jac))
    return results


def attend_kernel(count, place, gain_q, gain_k, q, k, v, near, far, kept, there, k_core, v_core,
                  first_kept, first_given, kv_last, q_core, q_row, part, part_there, logits, jac,
                  weight, qbuf, kbuf, vbuf, jbuf, pooled, sems, late, leave):
    mine, odd_layer, row, core, leading, here = (place[i] for i in (0, 1, 3, 4, 5, 6))
    edge = [jnp.where(place[i] == 1, NEG, 0.0) for i in (7, 8)]
    tokens = q.shape[0]
    width = STEP * HEAD
    steps = PER // STEP
    span = GROUP * tokens + 2 * ROW
    paired = pl.multiple_of((1 - odd_layer) * (span - ROW), ROW)
    other = pl.multiple_of(odd_layer * (span - ROW), ROW)

    def band(row, core, shift):
        return pl.ds(pl.multiple_of((row * 2 + core) * tokens + shift, ROW), tokens)

    def copies(step, kind, even=True):
        own = pl.ds(pl.multiple_of((mine * steps + step) * width, width), width)
        half = pl.ds(pl.multiple_of((row * steps + step) * width, width), width)
        cols = pl.ds(pl.multiple_of(step * width, width), width)
        if kind == 0:
            moves = [
                (q.at[:, own], band(row, core, 0)),
                (q_core.at[:, half], band(row, 1 - core, 0)),
                (q_row.at[0, :, cols], band(1 - row, core, 0)),
                (q_row.at[1, :, cols], band(1 - row, 1 - core, 0)),
            ]
        else:
            i = kind - 1
            raw, raw_core = ((k, k_core), (v, v_core))[i]
            first, shared = ((first_kept, kept), (first_given, there))[i if even else 1 - i]
            moves = [
                (raw.at[:, own], band(row, core, ROW)),
                (raw_core.at[:, half], band(row, 1 - core, ROW)),
                (kv_last.at[i, :, cols], band(1 - row, 1 - leading, ROW)),
                (near.at[i * ROW:(i + 1) * ROW, cols], pl.ds(paired, ROW)),
                (far.at[i * ROW:(i + 1) * ROW, cols], pl.ds(other, ROW)),
                (first.at[:, cols], band(1 - row, leading, ROW)),
                (shared.at[:, cols], pl.ds(span, GBLK)),
            ]
        buf = (qbuf, kbuf, vbuf)[kind]
        return [
            pltpu.make_async_copy(a, buf.at[step, b], sems.at[step, kind, n]) for n, (a, b) in enumerate(moves)
        ]

    def rows_of(readout):
        return pltpu.make_async_copy(readout, weight, late.at[0])

    def jacobian(step):
        heads = pl.ds(step * STEP, STEP)
        return pltpu.make_async_copy(jbuf.at[heads], jac.at[heads], leave.at[step])

    def start(step):
        for copy in copies(step, 0):
            copy.start()

        @pl.when(odd_layer == 0)
        def _():
            for copy in copies(step, 1, True) + copies(step, 2, True):
                copy.start()

        @pl.when(odd_layer == 1)
        def _():
            for copy in copies(step, 1, False) + copies(step, 2, False):
                copy.start()

    start(0)

    @pl.loop(0, steps)
    def _(step):
        @pl.when(step + 1 < steps)
        def _():
            start(step + 1)

        @pl.when((step == max(steps - 2, 0)) & (here == 1))
        def _():
            rows_of(part).start()

        @pl.when((step == max(steps - 2, 0)) & (here == 0))
        def _():
            rows_of(part_there).start()

        at = [pl.ds(mine * PER + step * STEP + i, 1) for i in range(STEP)]
        pair = [jnp.concatenate([gain[i, :] for i in at], axis=1) for gain in (gain_q, gain_k)]
        for copy in copies(step, 0) + copies(step, 1) + copies(step, 2):
            copy.wait()
        made = two_heads(qbuf[step], kbuf[step], vbuf[step], *pair, edge)
        for i in range(STEP):
            jbuf[step * STEP + i] = made[i][1]
        jacobian(step).start()
        pooled[pl.ds(step, 1), :] = jnp.concatenate([x for x, _ in made], axis=1)

    rows_of(part).wait()
    sums = jnp.concatenate([pooled[i:i + 1, :] for i in range(steps)], axis=1)
    made = dot(thirds(sums * (1.0 / count)), weight[...], NT)
    made = jnp.sum(made, axis=0, keepdims=True)
    made = jnp.concatenate([made, jnp.zeros((1, -made.shape[1] % HEAD), F32)], axis=1)
    made = jnp.concatenate([made[:, i:i + HEAD] for i in range(0, made.shape[1], HEAD)], axis=0)
    logits[...] = jnp.broadcast_to(made[None], logits.shape)
    for step in range(steps):
        jacobian(step).wait()


def attend(devices, count, place, gain_q, gain_k, q, k, v, near, far, kept, there, k_core, v_core, first_kept,
           first_given, kv_last, q_core, q_row, part, part_there):
    tokens = q.shape[0]
    keys = GROUP * tokens + 2 * ROW + GBLK
    width = STEP * HEAD
    steps = PER // STEP
    return pl.pallas_call(
        functools.partial(attend_kernel, count),
        out_shape=(
            jax.ShapeDtypeStruct((devices, -(-part.shape[0] // HEAD), HEAD), F32),
            jax.ShapeDtypeStruct((PER, HEAD, HEAD), F32),
        ),
        in_specs=[SMEM, VMEM, VMEM] + [HBM] * 16,
        out_specs=(VMEM, HBM),
        scratch_shapes=[
            pltpu.VMEM(part.shape, BF16),
            pltpu.VMEM((steps, GROUP * tokens, width), BF16),
            pltpu.VMEM((steps, keys, width), BF16),
            pltpu.VMEM((steps, keys, width), BF16),
            pltpu.VMEM((PER, HEAD, HEAD), F32),
            pltpu.VMEM((8, width), F32),
            pltpu.SemaphoreType.DMA((steps, 3, 7)),
            pltpu.SemaphoreType.DMA((1,)),
            pltpu.SemaphoreType.DMA((steps,)),
        ],
        compiler_params=ALONE,
        cost_estimate=pl.CostEstimate(flops=1_200_000_000, bytes_accessed=6_000_000, transcendentals=1_200_000),
        name="attend",
    )(place, gain_q, gain_k, q, k, v, near, far, kept, there, k_core, v_core, first_kept, first_given,
      kv_last, q_core, q_row, part, part_there)


def tail_kernel(count, classes, views, place, logits, part, part_there, jac, entropy, total, parts, weight, jbuf, sems):
    rows = weight.shape[0]
    pieces = [(i, min(HEAD, rows - i)) for i in range(0, rows, HEAD)]
    pieces = pieces[:-2] + [(pieces[-2][0], rows - pieces[-2][0])]

    def rows_of(readout):
        return [
            pltpu.make_async_copy(readout.at[pl.ds(i, n)], weight.at[pl.ds(i, n)], sems.at[j])
            for j, (i, n) in enumerate(pieces)
        ]

    gathered = pltpu.make_async_copy(logits, parts, sems.at[len(pieces) + 1])
    gathered.start()
    jacobian = pltpu.make_async_copy(jac, jbuf, sems.at[len(pieces)])
    jacobian.start()

    @pl.when(place[6] == 1)
    def _():
        for copy in rows_of(part):
            copy.start()

    @pl.when(place[6] == 0)
    def _():
        for copy in rows_of(part_there):
            copy.start()

    gathered.wait()
    per = parts.shape[0] // views
    tile = parts.shape[1:]
    index = lax.broadcasted_iota(jnp.int32, tile, 0) * HEAD + lax.broadcasted_iota(jnp.int32, tile, 1)
    valid = index < classes
    over_all = lambda f, x: f(f(x, axis=1, keepdims=True), axis=0, keepdims=True)
    mean = jnp.zeros(tile, F32)
    own = jnp.zeros(tile, F32)
    for i in range(views):
        x = jnp.where(valid, jnp.sum(parts[i * per:(i + 1) * per], axis=0), NEG)
        x = jnp.exp(x - over_all(jnp.max, x))
        x = x / over_all(jnp.sum, x)
        mean = mean + x
        own = jnp.where(place[2] == i, x, own)
    mean = mean * (1.0 / views)
    log = jnp.log(jnp.where(valid, mean, 1.0))
    entropy[...] = -over_all(jnp.sum, mean * log)
    upstream = (log + 1.0) * (-1.0 / views)
    dlogits = own * (upstream - over_all(jnp.sum, own * upstream))
    dlogits = jnp.concatenate([dlogits[i:i + 1] for i in range(tile[0])], axis=1)
    dlogits = thirds(dlogits)
    grad = jnp.zeros((dlogits.shape[0], weight.shape[1]), F32)
    for copy, (i, n) in zip(rows_of(part), pieces):
        copy.wait()
        grad = grad + dot(dlogits[:, i:i + n], weight[i:i + n, :], NN)
    grad = jnp.sum(grad, axis=0, keepdims=True) * (1.0 / count)
    jacobian.wait()
    rows = []
    for h in range(PER):
        g = thirds(grad[:, h * HEAD:(h + 1) * HEAD])
        j = jbuf[h]
        high = j.astype(BF16)
        low = (j - high.astype(F32)).astype(BF16)
        t = dot(g, high, NN) + dot(g, low, NN)
        rows.append(jnp.sum(t, axis=0, keepdims=True))
    rows.append(jnp.zeros((total.shape[0] - PER, HEAD), F32))
    total[...] = jnp.concatenate(rows, axis=0).astype(BF16)


def tail(count, classes, views, place, parts, part, part_there, jac):
    return pl.pallas_call(
        functools.partial(tail_kernel, count, classes, views),
        out_shape=(
            jax.ShapeDtypeStruct((1, 1), F32),
            jax.ShapeDtypeStruct((8, HEAD), BF16),
        ),
        in_specs=[SMEM] + [HBM] * 4,
        out_specs=(VMEM, VMEM),
        scratch_shapes=[
            pltpu.VMEM(parts.shape, F32),
            pltpu.VMEM(part.shape, BF16),
            pltpu.VMEM(jac.shape, F32),
            pltpu.SemaphoreType.DMA((-(-part.shape[0] // HEAD) + 1,)),
        ],
        compiler_params=ALONE,
        name="tail",
    )(place, parts, part, part_there, jac)


def finish_kernel(parts, gain_q, gain_k, q_grad, k_grad):
    for member in range(GROUP):
        total = parts[member].astype(F32)
        for i in range(member + GROUP, parts.shape[0], GROUP):
            total = total + parts[i].astype(F32)
        total = total[:PER] * SCALE
        at = slice(SHARES[member] * PER, (SHARES[member] + 1) * PER)
        q_grad[at, :] = total / gain_q[at, :]
        k_grad[at, :] = total / gain_k[at, :]


def finish(parts, gain_q, gain_k):
    shape = jax.ShapeDtypeStruct(gain_q.shape, F32)
    return pl.pallas_call(
        finish_kernel,
        out_shape=(shape, shape),
        in_specs=[VMEM] * 3,
        out_specs=(VMEM, VMEM),
        compiler_params=PARAMS,
        name="finish",
    )(parts, gain_q, gain_k)


def group_readout(readout, mine, group_rows):
    views = lax.axis_size("fsdp")
    layers = lax.axis_size("layer")
    rows = readout.shape[0]

    def cut(x, first):
        part = lax.dynamic_slice_in_dim(x, first * group_rows, group_rows, 0).T
        return lax.optimization_barrier(part)

    if views == 2 and rows % group_rows == 0:
        per = rows // group_rows
        part = cut(readout, mine % per)
        pairs = []
        for t in range(layers * GROUP):
            f = SHARES[t % GROUP] // per
            pairs.append((f * layers * GROUP + t, (1 - f) * layers * GROUP + t))
        there = lax.ppermute(part, ("fsdp", "layer", "row", "core"), pairs)
        return part, there, (lax.axis_index("fsdp") == mine // per).astype(jnp.int32)
    part = cut(lax.all_gather(readout, "fsdp", axis=0, tiled=True), mine)
    return part, part, jnp.int32(1)


def xor_layer(x, bit):
    return lax.ppermute(x, "layer", [(i, i ^ bit) for i in range(lax.axis_size("layer"))])


def other_core(x):
    return lax.ppermute(x, "core", [(0, 1), (1, 0)])


def other_row(x):
    return lax.ppermute(x, "row", [(0, 1), (1, 0)])


def every_device(x):
    return lax.all_to_all(x, ("fsdp", "layer", "row", "core"), 0, 0, tiled=True)


def after(x, *earlier):
    return lax.optimization_barrier((x, earlier))[0]


def body(queries, keys, values, readout, global_block, q_gain, k_gain):
    views = lax.axis_size("fsdp")
    layers = lax.axis_size("layer")
    core = lax.axis_index("core")
    row = lax.axis_index("row")
    mine = core * 2 + row
    theirs = core * 2 + 1 - row
    layer = lax.axis_index("layer")
    odd_layer = layer & 1
    q, k, v = queries[0], keys[0], values[0]
    tokens, channels = q.shape
    wide = channels // GROUP
    classes = readout.shape[1]
    count = tokens * layers * GROUP

    def columns(x, share):
        return lax.dynamic_slice_in_dim(x, share * wide, wide, 1)

    def kv_columns(share):
        return jnp.stack([columns(k, share), columns(v, share)])

    owner = global_block[0] // (tokens // GBLK)
    home = owner // GROUP
    leading = owner & 1
    leads = leading == core

    def half(x):
        return lax.dynamic_slice_in_dim(x, (1 - core) * 2 * wide, 2 * wide, 1)

    k_core, v_core = (other_core(x) for x in lax.optimization_barrier((half(k), half(v))))
    kv_core = jnp.stack([k_core, v_core])
    own = jnp.stack([columns(k, mine), columns(v, mine)])
    own_theirs = jnp.stack([columns(k, theirs), columns(v, theirs)])
    core_mine = lax.dynamic_slice_in_dim(kv_core, row * wide, wide, 2)
    core_theirs = lax.dynamic_slice_in_dim(kv_core, (1 - row) * wide, wide, 2)
    lead = jnp.where(leads, own_theirs, core_theirs)
    first_given = other_row(jnp.where(odd_layer == 0, lead[1], lead[0]))
    first_kept = other_row(jnp.where(odd_layer == 0, lead[0], lead[1]))
    kv_last = other_row(jnp.where(leads, core_theirs, own_theirs))
    part, part_there, here = group_readout(after(readout, v_core), mine, wide)
    place = jnp.stack([jnp.int32(x) for x in (mine, odd_layer, lax.axis_index("fsdp"), row, core, leading, here, layer == 0, layer == layers - 1)])
    outer = []
    for z in range(layers):
        other = z + 1 if z % 2 else z - 1
        if 0 <= other < layers:
            outer.append((z, other))

    near_row = (owner >> 1) & 1 == row
    held = jnp.where(leads, own, core_mine)
    given = jnp.where(near_row, jnp.where(odd_layer == 0, held[1], held[0]), first_given)
    kept = jnp.where(near_row, jnp.where(odd_layer == 0, held[0], held[1]), first_kept)
    given = xor_layer(given, 1)
    kept = jnp.where(layer == home, kept, given)
    kv_last = after(kv_last, kept)

    def band(index, rows):
        at_row, at_core = index >> 1, index & 1
        near = jnp.where(at_core == core, own[:, rows], core_mine[:, rows])
        keys = jnp.where(odd_layer == 0, first_kept[rows], first_given[rows])
        values = jnp.where(odd_layer == 0, first_given[rows], first_kept[rows])
        far_row = jnp.where(at_core == leading, jnp.stack([keys, values]), kv_last[:, rows])
        return jnp.where(at_row == row, near, far_row).reshape(2 * ROW, -1)

    first = band(0, slice(0, ROW))
    final = band(GROUP - 1, slice(tokens - ROW, tokens))
    near = xor_layer(jnp.where(odd_layer == 0, final, first), 1)
    far = lax.ppermute(jnp.where(odd_layer == 0, first, final), "layer", outer)
    part_there = after(part_there, near)
    q_late = after(q, first_given)
    q_core = other_core(half(after(q, v_core)))
    q_row = jnp.stack([columns(q_late, theirs), lax.dynamic_slice_in_dim(q_core, (1 - row) * wide, wide, 1)])
    q_row = other_row(q_row)
    bit = 2
    while bit < layers:
        kept = jnp.where(layer // bit == home // bit, kept, xor_layer(kept, bit))
        bit *= 2
    there = xor_layer(kept, 1)

    gain_q, gain_k = q_gain.reshape(-1, HEAD), k_gain.reshape(-1, HEAD)
    devices = views * layers * GROUP
    logits, jac = attend(
        devices, count, place, gain_q, gain_k, q, k, v, near, far, kept, there, k_core, v_core, first_kept,
        first_given, kv_last, q_core, q_row, part, part_there,
    )
    parts = every_device(logits)
    entropy, total = tail(count, classes, views, place, parts, part, part_there, jac)
    total = jnp.broadcast_to(total, (devices,) + total.shape)
    q_grad, k_grad = finish(every_device(total), gain_q, gain_k)
    return (entropy[0, 0], q_grad.reshape(-1), k_grad.reshape(-1))


def solution(mesh):
    views, toks = mesh.devices.shape
    grouped = Mesh(
        mesh.devices.reshape(views, toks // GROUP, GROUP // 2, 2), ("fsdp", "layer", "row", "core")
    )
    tok = ("layer", "row", "core")
    in_specs = (
        P("fsdp", tok, None),
        P("fsdp", tok, None),
        P("fsdp", tok, None),
        P("fsdp", None),
        P("fsdp"),
        P(),
        P(),
    )
    out_specs = (P(), P(), P())
    return jax.shard_map(body, mesh=grouped, in_specs=in_specs, out_specs=out_specs, check_vma=False)
```

```python
import functools

import jax
import jax.numpy as jnp
from jax import lax
from jax.experimental import pallas as pl
from jax.experimental.pallas import tpu as pltpu
from jax.sharding import Mesh, PartitionSpec as P

HEAD = 128
ROW = 64
GBLK = 128
GROUP = 4
PER = 6
STEP = 2
NEG = -1e30
SCALE = HEAD**-0.5
LOG2E = 1.4426950408889634
F32 = jnp.float32
BF16 = jnp.bfloat16
VMEM = pl.BlockSpec(memory_space=pltpu.VMEM)
SMEM = pl.BlockSpec(memory_space=pltpu.SMEM)
PARAMS = pltpu.CompilerParams(vmem_limit_bytes=16 * 1024 * 1024)
ALONE = pltpu.CompilerParams(vmem_limit_bytes=63 * 1024 * 1024)
HBM = pl.BlockSpec(memory_space=pltpu.HBM)

NN = (((1,), (0,)), ((), ()))
NT = (((1,), (1,)), ((), ()))

SHARES = (0, 2, 1, 3)


def dot(a, b, dims):
    return lax.dot_general(a, b, dims, preferred_element_type=F32)


def two(x):
    zero = jnp.zeros_like(x[0])
    return jnp.concatenate(
        [jnp.concatenate([x[0], zero], axis=1), jnp.concatenate([zero, x[1]], axis=1)], axis=0
    )


def centring():
    row = lax.broadcasted_iota(jnp.int32, (HEAD, HEAD), 0)
    col = lax.broadcasted_iota(jnp.int32, (HEAD, HEAD), 1)
    centre = ((row == col).astype(F32) - 1.0 / HEAD).astype(BF16)
    return two((centre, centre)), two(((row == col).astype(F32).astype(BF16),) * 2)


def unit_rows(x, centre):
    x = dot(x, centre, NN)
    parts = []
    for i in range(2):
        part = x[:, i * HEAD:(i + 1) * HEAD]
        variance = jnp.sum(part * part, axis=1, keepdims=True) * (1.0 / HEAD)
        parts.append(part * lax.rsqrt(variance + 1e-06))
    return jnp.concatenate(parts, axis=1)


def thirds(x):
    a = x.astype(BF16)
    rest = x - a.astype(F32)
    b = rest.astype(BF16)
    c = (rest - b.astype(F32)).astype(BF16)
    pad = jnp.zeros((13, x.shape[1]), BF16)
    return jnp.concatenate([a, b, c, pad], axis=0)


def prepare(q, keys, values, gain_q, gain_k):
    centre, eye = centring()
    tile = lambda x, t: x[t * HEAD:(t + 1) * HEAD]
    qn = [(unit_rows(tile(q, t), centre) * gain_q).astype(BF16) for t in range(GROUP)]
    qns = [jnp.transpose(x) for x in qn]
    kn = [(unit_rows(tile(keys, t), centre) * gain_k).astype(BF16) for t in range(GROUP + 2)]
    knt = [jnp.transpose(x) for x in kn]
    vt = dot(eye, values, NT).astype(BF16)
    vt = [vt[:, t * HEAD:(t + 1) * HEAD] for t in range(GROUP + 2)]
    return qn, qns, kn, knt, vt


def two_heads(prepared, edge):
    qn, qns, kn, knt, vt = prepared
    tile = lambda x, t: x[t * HEAD:(t + 1) * HEAD]
    side = lambda x, i: x[:, i * HEAD:(i + 1) * HEAD]
    beside = lambda *parts: jnp.concatenate(parts, axis=1)
    below = lambda *parts: jnp.concatenate(parts, axis=0)
    qnt = [two((tile(x, 0), tile(x, 1))) for x in qns]

    last = GROUP + 1
    attn = []
    for b in range(GROUP):
        scores = dot(below(kn[b], kn[b + 1], kn[last]), qnt[b], NN)
        if b == 0:
            scores = below(scores[:ROW] + edge[0], scores[ROW:])
        if b == GROUP - 1:
            at = 2 * HEAD
            scores = below(scores[:at - ROW], scores[at - ROW:at] + edge[1], scores[at:])
        top = jnp.max(scores, axis=0, keepdims=True)
        expo = jnp.exp2((scores - top) * (SCALE * LOG2E))
        attn.append((expo * (1.0 / jnp.sum(expo, axis=0, keepdims=True))).astype(BF16))

    zero = jnp.zeros((HEAD, HEAD), BF16)
    results = []
    for i in range(2):
        both = [below(tile(knt[t], i), tile(vt[t], i)) for t in range(GROUP + 2)]
        back = [None] * (GROUP + 2)
        outs, negs = [], []
        for b in range(0, GROUP, 2):
            one, other = side(attn[b], i), side(attn[b + 1], i)
            pair = below(
                beside(tile(one, 0), zero),
                beside(tile(one, 1), tile(other, 0)),
                beside(zero, tile(other, 1)),
                beside(tile(one, 2), tile(other, 2)),
            )
            made = dot(beside(both[b], both[b + 1], both[b + 2], both[last]), pair, NN)
            queries = below(side(qn[b], i), side(qn[b + 1], i))
            outs.append(made[HEAD:])
            negs.append(beside(tile(qns[b], i), tile(qns[b + 1], i)) * made[:HEAD].astype(BF16))
            moved = dot(pair, queries, NN)
            for n, t in enumerate((b, b + 1, b + 2, last)):
                piece = tile(moved, n)
                back[t] = piece if back[t] is None else back[t] + piece
        moved = [side(kn[t], i) * back[t].astype(BF16) for t in range(GROUP + 2)]
        jac = dot(beside(*[tile(v, i) for v in vt]), below(*moved), NN)
        jac = jac - dot(beside(*[o.astype(BF16) for o in outs]), beside(*negs), NT)
        sums = outs[0] + outs[1]
        sums = side(sums, 0) + side(sums, 1)
        results.append((jnp.sum(jnp.transpose(sums), axis=0, keepdims=True), jac))
    return results


def attend_kernel(count, place, gain_q, gain_k, q, k, v, near, far, kept, there, k_core, v_core,
                  first_kept, first_given, kv_last, q_core, q_row, part, part_there, logits, jac,
                  weight, qbuf, kbuf, vbuf, jbuf, pooled, sems, late, leave):
    mine, odd_layer, row, core, leading, here = (place[i] for i in (0, 1, 3, 4, 5, 6))
    edge = [jnp.where(place[i] == 1, NEG, 0.0) for i in (7, 8)]
    tokens = q.shape[0]
    width = STEP * HEAD
    wide = PER * HEAD
    steps = PER // STEP
    span = GROUP * tokens + 2 * ROW
    paired = pl.multiple_of((1 - odd_layer) * (span - ROW), ROW)
    other = pl.multiple_of(odd_layer * (span - ROW), ROW)

    def band(row, core, shift):
        return pl.ds(pl.multiple_of((row * 2 + core) * tokens + shift, ROW), tokens)

    def copies(kind, even=True):
        own = pl.ds(pl.multiple_of(mine * wide, wide), wide)
        half = pl.ds(pl.multiple_of(row * wide, wide), wide)
        if kind == 0:
            moves = [
                (q.at[:, own], band(row, core, 0)),
                (q_core.at[:, half], band(row, 1 - core, 0)),
                (q_row.at[0], band(1 - row, core, 0)),
                (q_row.at[1], band(1 - row, 1 - core, 0)),
            ]
        else:
            i = kind - 1
            raw, raw_core = ((k, k_core), (v, v_core))[i]
            first, shared = ((first_kept, kept), (first_given, there))[i if even else 1 - i]
            moves = [
                (raw.at[:, own], band(row, core, ROW)),
                (raw_core.at[:, half], band(row, 1 - core, ROW)),
                (kv_last.at[i], band(1 - row, 1 - leading, ROW)),
                (near.at[i * ROW:(i + 1) * ROW], pl.ds(paired, ROW)),
                (far.at[i * ROW:(i + 1) * ROW], pl.ds(other, ROW)),
                (first, band(1 - row, leading, ROW)),
                (shared, pl.ds(span, GBLK)),
            ]
        buf = (qbuf, kbuf, vbuf)[kind]
        return [pltpu.make_async_copy(a, buf.at[b], sems.at[kind, n]) for n, (a, b) in enumerate(moves)]

    def rows_of(readout):
        return pltpu.make_async_copy(readout, weight, late.at[0])

    def jacobian(step):
        heads = pl.ds(step * STEP, STEP)
        return pltpu.make_async_copy(jbuf.at[heads], jac.at[heads], leave.at[step])

    for copy in copies(0):
        copy.start()

    @pl.when(odd_layer == 0)
    def _():
        for copy in copies(1, True) + copies(2, True):
            copy.start()

    @pl.when(odd_layer == 1)
    def _():
        for copy in copies(1, False) + copies(2, False):
            copy.start()

    for copy in copies(0) + copies(1) + copies(2):
        copy.wait()

    @pl.when(here == 1)
    def _():
        rows_of(part).start()

    @pl.when(here == 0)
    def _():
        rows_of(part_there).start()

    def ready(step):
        at = [pl.ds(mine * PER + step * STEP + i, 1) for i in range(STEP)]
        pair = [jnp.concatenate([gain[i, :] for i in at], axis=1) for gain in (gain_q, gain_k)]
        cols = slice(step * width, (step + 1) * width)
        return prepare(qbuf[:, cols], kbuf[:, cols], vbuf[:, cols], *pair)

    prepared = ready(0)
    for step in range(steps):
        following = ready(step + 1) if step + 1 < steps else None
        made = two_heads(prepared, edge)
        for i in range(STEP):
            jbuf[step * STEP + i] = made[i][1]
        jacobian(step).start()
        pooled[step:step + 1, :] = jnp.concatenate([x for x, _ in made], axis=1)
        prepared = following

    rows_of(part).wait()
    sums = jnp.concatenate([pooled[i:i + 1, :] for i in range(steps)], axis=1)
    made = dot(thirds(sums * (1.0 / count)), weight[...], NT)
    made = jnp.sum(made, axis=0, keepdims=True)
    made = jnp.concatenate([made, jnp.zeros((1, -made.shape[1] % HEAD), F32)], axis=1)
    made = jnp.concatenate([made[:, i:i + HEAD] for i in range(0, made.shape[1], HEAD)], axis=0)
    logits[...] = jnp.broadcast_to(made[None], logits.shape)
    for step in range(steps):
        jacobian(step).wait()


def attend(devices, count, place, gain_q, gain_k, q, k, v, near, far, kept, there, k_core, v_core, first_kept,
           first_given, kv_last, q_core, q_row, part, part_there):
    tokens = q.shape[0]
    keys = GROUP * tokens + 2 * ROW + GBLK
    width = STEP * HEAD
    steps = PER // STEP
    return pl.pallas_call(
        functools.partial(attend_kernel, count),
        out_shape=(
            jax.ShapeDtypeStruct((devices, -(-part.shape[0] // HEAD), HEAD), F32),
            jax.ShapeDtypeStruct((PER, HEAD, HEAD), F32),
        ),
        in_specs=[SMEM, VMEM, VMEM] + [HBM] * 16,
        out_specs=(VMEM, HBM),
        scratch_shapes=[
            pltpu.VMEM(part.shape, BF16),
            pltpu.VMEM((GROUP * tokens, PER * HEAD), BF16),
            pltpu.VMEM((keys, PER * HEAD), BF16),
            pltpu.VMEM((keys, PER * HEAD), BF16),
            pltpu.VMEM((PER, HEAD, HEAD), F32),
            pltpu.VMEM((8, width), F32),
            pltpu.SemaphoreType.DMA((3, 7)),
            pltpu.SemaphoreType.DMA((1,)),
            pltpu.SemaphoreType.DMA((steps,)),
        ],
        compiler_params=ALONE,
        cost_estimate=pl.CostEstimate(flops=1_200_000_000, bytes_accessed=6_000_000, transcendentals=1_200_000),
        name="attend",
    )(place, gain_q, gain_k, q, k, v, near, far, kept, there, k_core, v_core, first_kept, first_given,
      kv_last, q_core, q_row, part, part_there)


def tail_kernel(count, classes, views, place, logits, part, part_there, jac, entropy, total, parts, weight, jbuf, sems):
    rows = weight.shape[0]
    pieces = [(i, min(HEAD, rows - i)) for i in range(0, rows, HEAD)]
    pieces = pieces[:-2] + [(pieces[-2][0], rows - pieces[-2][0])]

    def rows_of(readout):
        return [
            pltpu.make_async_copy(readout.at[pl.ds(i, n)], weight.at[pl.ds(i, n)], sems.at[j])
            for j, (i, n) in enumerate(pieces)
        ]

    gathered = pltpu.make_async_copy(logits, parts, sems.at[len(pieces) + 1])
    gathered.start()
    jacobian = pltpu.make_async_copy(jac, jbuf, sems.at[len(pieces)])
    jacobian.start()

    @pl.when(place[6] == 1)
    def _():
        for copy in rows_of(part):
            copy.start()

    @pl.when(place[6] == 0)
    def _():
        for copy in rows_of(part_there):
            copy.start()

    gathered.wait()
    per = parts.shape[0] // views
    tile = parts.shape[1:]
    index = lax.broadcasted_iota(jnp.int32, tile, 0) * HEAD + lax.broadcasted_iota(jnp.int32, tile, 1)
    valid = index < classes
    over_all = lambda f, x: f(f(x, axis=1, keepdims=True), axis=0, keepdims=True)
    mean = jnp.zeros(tile, F32)
    own = jnp.zeros(tile, F32)
    for i in range(views):
        x = jnp.where(valid, jnp.sum(parts[i * per:(i + 1) * per], axis=0), NEG)
        x = jnp.exp(x - over_all(jnp.max, x))
        x = x / over_all(jnp.sum, x)
        mean = mean + x
        own = jnp.where(place[2] == i, x, own)
    mean = mean * (1.0 / views)
    log = jnp.log(jnp.where(valid, mean, 1.0))
    entropy[...] = -over_all(jnp.sum, mean * log)
    upstream = (log + 1.0) * (-1.0 / views)
    dlogits = own * (upstream - over_all(jnp.sum, own * upstream))
    dlogits = jnp.concatenate([dlogits[i:i + 1] for i in range(tile[0])], axis=1)
    dlogits = thirds(dlogits)
    grad = jnp.zeros((dlogits.shape[0], weight.shape[1]), F32)
    for copy, (i, n) in zip(rows_of(part), pieces):
        copy.wait()
        grad = grad + dot(dlogits[:, i:i + n], weight[i:i + n, :], NN)
    grad = jnp.sum(grad, axis=0, keepdims=True) * (1.0 / count)
    jacobian.wait()
    rows = []
    for h in range(PER):
        g = thirds(grad[:, h * HEAD:(h + 1) * HEAD])
        j = jbuf[h]
        high = j.astype(BF16)
        low = (j - high.astype(F32)).astype(BF16)
        t = dot(g, high, NN) + dot(g, low, NN)
        rows.append(jnp.sum(t, axis=0, keepdims=True))
    rows.append(jnp.zeros((total.shape[0] - PER, HEAD), F32))
    total[...] = jnp.concatenate(rows, axis=0).astype(BF16)


def tail(count, classes, views, place, parts, part, part_there, jac):
    return pl.pallas_call(
        functools.partial(tail_kernel, count, classes, views),
        out_shape=(
            jax.ShapeDtypeStruct((1, 1), F32),
            jax.ShapeDtypeStruct((8, HEAD), BF16),
        ),
        in_specs=[SMEM] + [HBM] * 4,
        out_specs=(VMEM, VMEM),
        scratch_shapes=[
            pltpu.VMEM(parts.shape, F32),
            pltpu.VMEM(part.shape, BF16),
            pltpu.VMEM(jac.shape, F32),
            pltpu.SemaphoreType.DMA((-(-part.shape[0] // HEAD) + 1,)),
        ],
        compiler_params=ALONE,
        name="tail",
    )(place, parts, part, part_there, jac)


def finish_kernel(parts, gain_q, gain_k, q_grad, k_grad):
    for member in range(GROUP):
        total = parts[member].astype(F32)
        for i in range(member + GROUP, parts.shape[0], GROUP):
            total = total + parts[i].astype(F32)
        total = total[:PER] * SCALE
        at = slice(SHARES[member] * PER, (SHARES[member] + 1) * PER)
        q_grad[at, :] = total / gain_q[at, :]
        k_grad[at, :] = total / gain_k[at, :]


def finish(parts, gain_q, gain_k):
    shape = jax.ShapeDtypeStruct(gain_q.shape, F32)
    return pl.pallas_call(
        finish_kernel,
        out_shape=(shape, shape),
        in_specs=[VMEM] * 3,
        out_specs=(VMEM, VMEM),
        compiler_params=PARAMS,
        name="finish",
    )(parts, gain_q, gain_k)


def group_readout(readout, mine, group_rows):
    views = lax.axis_size("fsdp")
    layers = lax.axis_size("layer")
    rows = readout.shape[0]

    def cut(x, first):
        part = lax.dynamic_slice_in_dim(x, first * group_rows, group_rows, 0).T
        return lax.optimization_barrier(part)

    if views == 2 and rows % group_rows == 0:
        per = rows // group_rows
        part = cut(readout, mine % per)
        pairs = []
        for t in range(layers * GROUP):
            f = SHARES[t % GROUP] // per
            pairs.append((f * layers * GROUP + t, (1 - f) * layers * GROUP + t))
        there = lax.ppermute(part, ("fsdp", "layer", "row", "core"), pairs)
        return part, there, (lax.axis_index("fsdp") == mine // per).astype(jnp.int32)
    part = cut(lax.all_gather(readout, "fsdp", axis=0, tiled=True), mine)
    return part, part, jnp.int32(1)


def xor_layer(x, bit):
    return lax.ppermute(x, "layer", [(i, i ^ bit) for i in range(lax.axis_size("layer"))])


def other_core(x):
    return lax.ppermute(x, "core", [(0, 1), (1, 0)])


def other_row(x):
    return lax.ppermute(x, "row", [(0, 1), (1, 0)])


def every_device(x):
    return lax.all_to_all(x, ("fsdp", "layer", "row", "core"), 0, 0, tiled=True)


def after(x, *earlier):
    return lax.optimization_barrier((x, earlier))[0]


def body(queries, keys, values, readout, global_block, q_gain, k_gain):
    views = lax.axis_size("fsdp")
    layers = lax.axis_size("layer")
    core = lax.axis_index("core")
    row = lax.axis_index("row")
    mine = core * 2 + row
    theirs = core * 2 + 1 - row
    layer = lax.axis_index("layer")
    odd_layer = layer & 1
    q, k, v = queries[0], keys[0], values[0]
    tokens, channels = q.shape
    wide = channels // GROUP
    classes = readout.shape[1]
    count = tokens * layers * GROUP

    def columns(x, share):
        return lax.dynamic_slice_in_dim(x, share * wide, wide, 1)

    def kv_columns(share):
        return jnp.stack([columns(k, share), columns(v, share)])

    owner = global_block[0] // (tokens // GBLK)
    home = owner // GROUP
    leading = owner & 1
    leads = leading == core

    def half(x):
        return lax.dynamic_slice_in_dim(x, (1 - core) * 2 * wide, 2 * wide, 1)

    k_core, v_core = (other_core(x) for x in lax.optimization_barrier((half(k), half(v))))
    kv_core = jnp.stack([k_core, v_core])
    own = jnp.stack([columns(k, mine), columns(v, mine)])
    own_theirs = jnp.stack([columns(k, theirs), columns(v, theirs)])
    core_mine = lax.dynamic_slice_in_dim(kv_core, row * wide, wide, 2)
    core_theirs = lax.dynamic_slice_in_dim(kv_core, (1 - row) * wide, wide, 2)
    lead = jnp.where(leads, own_theirs, core_theirs)
    first_given = other_row(jnp.where(odd_layer == 0, lead[1], lead[0]))
    first_kept = other_row(jnp.where(odd_layer == 0, lead[0], lead[1]))
    kv_last = other_row(jnp.where(leads, core_theirs, own_theirs))
    part, part_there, here = group_readout(after(readout, v_core), mine, wide)
    place = jnp.stack([jnp.int32(x) for x in (mine, odd_layer, lax.axis_index("fsdp"), row, core, leading, here, layer == 0, layer == layers - 1)])
    outer = []
    for z in range(layers):
        other = z + 1 if z % 2 else z - 1
        if 0 <= other < layers:
            outer.append((z, other))

    near_row = (owner >> 1) & 1 == row
    held = jnp.where(leads, own, core_mine)
    given = jnp.where(near_row, jnp.where(odd_layer == 0, held[1], held[0]), first_given)
    kept = jnp.where(near_row, jnp.where(odd_layer == 0, held[0], held[1]), first_kept)
    given = xor_layer(given, 1)
    kept = jnp.where(layer == home, kept, given)
    kv_last = after(kv_last, kept)

    def band(index, rows):
        at_row, at_core = index >> 1, index & 1
        near = jnp.where(at_core == core, own[:, rows], core_mine[:, rows])
        keys = jnp.where(odd_layer == 0, first_kept[rows], first_given[rows])
        values = jnp.where(odd_layer == 0, first_given[rows], first_kept[rows])
        far_row = jnp.where(at_core == leading, jnp.stack([keys, values]), kv_last[:, rows])
        return jnp.where(at_row == row, near, far_row).reshape(2 * ROW, -1)

    first = band(0, slice(0, ROW))
    final = band(GROUP - 1, slice(tokens - ROW, tokens))
    near = xor_layer(jnp.where(odd_layer == 0, final, first), 1)
    far = lax.ppermute(jnp.where(odd_layer == 0, first, final), "layer", outer)
    part_there = after(part_there, near)
    q_late = after(q, first_given)
    q_core = other_core(half(after(q, v_core)))
    q_row = jnp.stack([columns(q_late, theirs), lax.dynamic_slice_in_dim(q_core, (1 - row) * wide, wide, 1)])
    q_row = other_row(q_row)
    bit = 2
    while bit < layers:
        kept = jnp.where(layer // bit == home // bit, kept, xor_layer(kept, bit))
        bit *= 2
    there = xor_layer(kept, 1)

    gain_q, gain_k = q_gain.reshape(-1, HEAD), k_gain.reshape(-1, HEAD)
    devices = views * layers * GROUP
    logits, jac = attend(
        devices, count, place, gain_q, gain_k, q, k, v, near, far, kept, there, k_core, v_core, first_kept,
        first_given, kv_last, q_core, q_row, part, part_there,
    )
    parts = every_device(logits)
    entropy, total = tail(count, classes, views, place, parts, part, part_there, jac)
    total = jnp.broadcast_to(total, (devices,) + total.shape)
    q_grad, k_grad = finish(every_device(total), gain_q, gain_k)
    return (entropy[0, 0], q_grad.reshape(-1), k_grad.reshape(-1))


def solution(mesh):
    views, toks = mesh.devices.shape
    grouped = Mesh(
        mesh.devices.reshape(views, toks // GROUP, GROUP // 2, 2), ("fsdp", "layer", "row", "core")
    )
    tok = ("layer", "row", "core")
    in_specs = (
        P("fsdp", tok, None),
        P("fsdp", tok, None),
        P("fsdp", tok, None),
        P("fsdp", None),
        P("fsdp"),
        P(),
        P(),
    )
    out_specs = (P(), P(), P())
    return jax.shard_map(body, mesh=grouped, in_specs=in_specs, out_specs=out_specs, check_vma=False)
```
